32 devices in a mesh: groups: 2 (over y), ctx: 4 (over z), head: 2 (over x), section: 2 (over core).
Axes of the slice: x: 2, y: 2, z: 4, core: 2. Of those that a mesh axis runs over, the one named last changes fastest.
Arguments:
- tokens: bfloat16 [1024, 8192], P(('groups', 'ctx'), ('head', 'section')), parts along dimension 0, may hold values from -6 to 6
- norm_gain: bfloat16 [8192], replicated, may hold values from 0.099609375 to 1.8984375
- w_qkv: bfloat16 [8192, 10240], P('ctx', ('head', 'section')), may hold values from -0.0625 to 0.0625
- prefix_kv: bfloat16 [4096, 8, 256], P(('groups', 'ctx'), ('head', 'section')), parts along dimension 0, may hold values from -200 to 200
- prefix_counts: int32 [8], P(('groups', 'ctx')), parts along dimension 0, may hold values from 0 to 4, as said below
- span_offset: int32 [2], P('groups'), parts along dimension 0, may hold values from 32 to 95
- handoff_slots: int32 [8], P(('groups', 'ctx')), parts along dimension 0, may hold values from 0 to 15, as said below
Outputs:
- attended: bfloat16 [1024, 8192], P(('groups', 'ctx'), ('head', 'section')), parts along dimension 0
- decode_cache: bfloat16 [4096, 8, 256], P(('groups', 'ctx'), ('head', 'section')), parts along dimension 0
The draws below stay inside these ranges and needn't reach their ends.
There are 2 independent parts, one for each index of `groups`. The reference program is written for one: setup_inputs(seed, part) draws one part's arguments, and reference() takes and returns one part's arrays. A program takes and returns all parts, laid end to end along the dimension named above; an argument that names none is the same for every part. Nothing has to cross between parts.
Inputs may be any that keep to these rules, and one draw needn't show every extreme that they name: `prefix_counts`: some index of ctx holds all 4 blocks. `handoff_slots`: distinct values; slot s belongs to index s // 4 of ctx; a quarter of the indices of ctx receive blocks, each of them in all of its 4 slots.
All inputs are finite; a program needn't handle non-finite values.
Results may differ from the reference program's by a relative error of at most 0.007.
The reference program's roundings to bfloat16 on the way (of `normed`, `queries` and `new_pairs`) count: a program that leaves them out, or rounds other values in their place, can miss the bound.
Values may be sent and summed in bfloat16 or wider, within the bound.
A program may use at most 128 MiB of HBM per device.

```python
import math
import jax
import jax.numpy as jnp
from jax import lax

D = 8192
KVH = 8
HEAD_DIM = 128
GROUP = 8
BLK = 128
TOK_DEV = 128
PB_DEV = 4
TOKENS = 512
NBLK = 4
SLOTS = 4
COLS = 10240
N_CTX = 4


def draw_prefix_kv(key, part):
    key = jax.random.fold_in(key, 7)
    key_main = jax.random.fold_in(key, 0)
    prefix_rows = N_CTX * PB_DEV * BLK
    entries = jax.random.truncated_normal(key_main, -5.0, 5.0, (prefix_rows, KVH, 2 * HEAD_DIM), jnp.float32)
    return entries.astype(jnp.bfloat16)


def draw_prefix_counts(key, part):
    key = jax.random.fold_in(key, 11)
    key_counts, key_full = jax.random.split(key)
    counts = jax.random.randint(key_counts, (N_CTX,), 0, PB_DEV + 1)
    full_index = jax.random.randint(key_full, (), 0, N_CTX)
    return jnp.where(jnp.arange(N_CTX) == full_index, PB_DEV, counts).astype(jnp.int32)


def draw_handoff_slots(key, part):
    key = jax.random.fold_in(key, 12)
    key_recv, key_order = jax.random.split(key)
    others = jax.random.permutation(key_recv, N_CTX - 1)[:N_CTX // 4 - 1]
    receivers = jnp.concatenate([jnp.full((1,), N_CTX - 1, jnp.int32), others.astype(jnp.int32)])
    order = jax.random.permutation(key_order, NBLK)
    return (receivers[order // SLOTS] * SLOTS + order % SLOTS).astype(jnp.int32)


def level_of(rng, extent, pieces, least, largest):
    def one(position, blocks):
        steps = jax.random.uniform(jax.random.fold_in(jax.random.fold_in(rng, 6), position), (blocks,), jnp.float32, least / len(pieces), largest / len(pieces))
        return jnp.repeat(jnp.exp(steps), extent[position] // blocks).reshape((-1,) + (1,) * (len(extent) - position - 1))

    factor_of = one(*pieces[0])
    for cut in pieces[1:]:
        factor_of = factor_of * one(*cut)
    return factor_of


def normal_values(own_key, extent, spread, most, cuts=(), kind=jnp.bfloat16):
    values = jax.random.normal(own_key, extent, jnp.float32) * spread
    if len(cuts) > 0:
        values = level_of(own_key, extent, cuts, -0.22, 0.18) * values
    return jnp.clip(values, min=-most, max=most).astype(kind)


def setup_inputs(seed: int = 0, part: int = 0) -> dict:
    keys = jax.random.split(jax.random.key(seed), 8)
    part_splits = jax.random.split(jax.random.fold_in(keys[7], part), 8)
    return {
        "tokens": normal_values(part_splits[0], (TOKENS, D), 1.0, 6.0, ((0, 4), (1, 4))),
        "norm_gain": jnp.clip(1.0 + 0.18 * jax.random.normal(keys[1], (D,), jnp.float32), 0.099609375, 1.8984375).astype(jnp.bfloat16),
        "w_qkv": normal_values(keys[2], (D, COLS), D ** -0.5, 0.0625, ((0, 4), (1, 4))),
        "prefix_kv": draw_prefix_kv(jax.random.fold_in(jax.random.fold_in(keys[7], part), 71), part),
        "prefix_counts": draw_prefix_counts(jax.random.fold_in(jax.random.fold_in(keys[7], part), 71), part),
        "span_offset": jax.random.randint(part_splits[5], (1,), 32, 96).astype(jnp.int32),
        "handoff_slots": draw_handoff_slots(jax.random.fold_in(jax.random.fold_in(keys[7], part), 71), part),
    }


ROPE_BASE = 500000.0
NORM_EPS = 1e-05

def rotate(vectors, positions):
    half_dim = vectors.shape[-1] // 2
    frequency = ROPE_BASE ** (-(jnp.arange(half_dim, dtype=jnp.float32) * 2.0) / vectors.shape[-1])
    angles = positions[:, None] * frequency[None, :]
    view_shape = (vectors.shape[0],) + (1,) * (vectors.ndim - 2) + (half_dim,)
    cosines = jnp.cos(angles).reshape(view_shape)
    sine_part = jnp.sin(angles).reshape(view_shape)
    lower_part = vectors[..., :half_dim]
    upper_part = vectors[..., half_dim:]
    return jnp.concatenate([lower_part * cosines - upper_part * sine_part, upper_part * cosines + lower_part * sine_part], -1)

def reference(tokens, norm_gain, w_qkv, prefix_kv, prefix_counts, span_offset, handoff_slots):
    row_count = tokens.shape[0]
    values = tokens.astype(jnp.float32)
    scale_row = lax.rsqrt(lax.optimization_barrier(jnp.mean(values * values, -1, keepdims=True)) + NORM_EPS)
    normed = (values * scale_row * norm_gain.astype(jnp.float32)).astype(jnp.bfloat16)
    projected = jnp.dot(normed, w_qkv, preferred_element_type=jnp.float32).reshape(row_count, KVH, GROUP + 2, HEAD_DIM)
    positions = (span_offset[0] * BLK + jnp.arange(row_count, dtype=jnp.int32)).astype(jnp.float32)
    queries = rotate(projected[:, :, :GROUP], positions).astype(jnp.bfloat16)
    keys_new = rotate(projected[:, :, GROUP], positions).astype(jnp.bfloat16)
    values_new = projected[:, :, GROUP + 1].astype(jnp.bfloat16)
    new_pairs = jnp.concatenate([keys_new, values_new], -1)
    prefix_rows = prefix_kv.shape[0]
    per_dev = PB_DEV * BLK
    slot_index = jnp.arange(prefix_rows, dtype=jnp.int32)
    live_rows = slot_index % per_dev < jnp.repeat(prefix_counts, per_dev) * BLK
    keys_all = jnp.concatenate([prefix_kv[:, :, :HEAD_DIM], keys_new], 0).astype(jnp.float32)
    values_all = jnp.concatenate([prefix_kv[:, :, HEAD_DIM:], values_new], 0).astype(jnp.float32)
    key_pos = jnp.arange(row_count, dtype=jnp.int32)
    scale = 1.0 / math.sqrt(HEAD_DIM)

    def one_block(block_start):
        query_block = lax.dynamic_slice_in_dim(queries, block_start, TOK_DEV, 0).astype(jnp.float32)
        query_pos = block_start + jnp.arange(TOK_DEV, dtype=jnp.int32)
        causal = key_pos[None, :] <= query_pos[:, None]
        visible = jnp.concatenate([jnp.broadcast_to(live_rows[None, :], (TOK_DEV, prefix_rows)), causal], 1)[:, None, None, :]
        scores = jnp.einsum('qhgd,khd->qhgk', query_block, keys_all) * scale
        running_max = lax.optimization_barrier(jnp.max(jnp.where(visible, scores, -1e+30), -1, keepdims=True))
        weights = jnp.where(visible, jnp.exp(scores - running_max), 0.0)
        totals = lax.optimization_barrier(jnp.sum(weights, -1))
        rounded = lax.optimization_barrier(weights.astype(jnp.bfloat16)).astype(jnp.float32)
        blended = jnp.einsum('qhgk,khd->qhgd', rounded, values_all)
        return blended / totals[..., None]
    block_starts = jnp.arange(0, row_count, TOK_DEV, dtype=jnp.int32)
    blocks = lax.map(one_block, block_starts)
    attended = blocks.reshape(row_count, KVH * GROUP * HEAD_DIM).astype(jnp.bfloat16)
    decode_rows = jnp.zeros((N_CTX * SLOTS, BLK, KVH, 2 * HEAD_DIM), jnp.bfloat16)
    decode_rows = decode_rows.at[handoff_slots].set(new_pairs.reshape(row_count // BLK, BLK, KVH, 2 * HEAD_DIM))
    return (attended, decode_rows.reshape(N_CTX * SLOTS * BLK, KVH, 2 * HEAD_DIM))
```

```python
import math

import jax
import jax.numpy as jnp
from jax import lax
from jax.sharding import PartitionSpec as P

HEAD_DIM = 128
GROUP = 8
BLK = 128


ROPE_BASE = 500000.0
NORM_EPS = 1e-05


def rotate(vectors, positions):
    half_dim = vectors.shape[-1] // 2
    frequency = ROPE_BASE ** (-(jnp.arange(half_dim, dtype=jnp.float32) * 2.0) / vectors.shape[-1])
    angles = positions[:, None] * frequency[None, :]
    view_shape = (vectors.shape[0],) + (1,) * (vectors.ndim - 2) + (half_dim,)
    cosines = jnp.cos(angles).reshape(view_shape)
    sine_part = jnp.sin(angles).reshape(view_shape)
    lower_part = vectors[..., :half_dim]
    upper_part = vectors[..., half_dim:]
    return jnp.concatenate(
        [
            lower_part * cosines - upper_part * sine_part,
            upper_part * cosines + lower_part * sine_part,
        ],
        -1,
    )


def fresh_state(row_count, head_count):
    return (
        jnp.full((row_count, head_count, GROUP), -1e30, jnp.float32),
        jnp.zeros((row_count, head_count, GROUP), jnp.float32),
        jnp.zeros((row_count, head_count, GROUP, HEAD_DIM), jnp.float32),
    )


def advance(states_now, query_set, key_rows, value_rows, visible):
    running_max, totals, weighted_sum = states_now
    scores = jnp.einsum(
        "rhgd,khd->rhgk", query_set, key_rows, preferred_element_type=jnp.float32
    ) * (1.0 / math.sqrt(HEAD_DIM))
    visible_map = visible[:, None, None, :]
    new_max = jnp.maximum(running_max, jnp.max(jnp.where(visible_map, scores, -1e30), -1))
    shrink_by = jnp.exp(running_max - new_max)
    weights = jnp.where(visible_map, jnp.exp(scores - new_max[..., None]), 0.0)
    totals = totals * shrink_by + jnp.sum(weights, -1)
    weighted_sum = weighted_sum * shrink_by[..., None] + jnp.einsum(
        "rhgk,khd->rhgd",
        weights.astype(jnp.bfloat16),
        value_rows,
        preferred_element_type=jnp.float32,
    )
    return (new_max, totals, weighted_sum)


def finish(states_now):
    running_max, totals, weighted_sum = states_now
    blended = weighted_sum / totals[..., None]
    return blended.reshape(blended.shape[0], -1).astype(jnp.bfloat16)


def local(tokens, norm_gain, w_qkv, prefix_kv, prefix_counts, span_offset, handoff_slots):
    row_count = tokens.shape[0]
    device = lax.axis_index("ctx")
    values = tokens.astype(jnp.float32)
    square_sum = lax.psum(jnp.sum(values * values, -1, keepdims=True), ("head", "section"))
    scale_row = lax.rsqrt(square_sum / norm_gain.shape[0] + NORM_EPS)
    hs = lax.axis_index("head") * lax.axis_size("section") + lax.axis_index("section")
    gain = lax.dynamic_slice_in_dim(norm_gain, hs * tokens.shape[1], tokens.shape[1], 0)
    normed = (values * scale_row * gain.astype(jnp.float32)).astype(jnp.bfloat16)
    normed = lax.all_gather(normed, ("head", "section"), axis=1, tiled=True)
    normed = lax.all_to_all(normed, "ctx", split_axis=1, concat_axis=0, tiled=True)
    proj_width = w_qkv.shape[1]
    partial = jnp.dot(normed, w_qkv, preferred_element_type=jnp.float32)
    projected = lax.psum_scatter(partial, "ctx", scatter_dimension=0, tiled=True)
    head_count = proj_width // ((GROUP + 2) * HEAD_DIM)
    projected = projected.reshape(row_count, head_count, GROUP + 2, HEAD_DIM)
    local_pos = device * row_count + jnp.arange(row_count, dtype=jnp.int32)
    positions = (span_offset[0] * BLK + local_pos).astype(jnp.float32)
    queries = rotate(projected[:, :, :GROUP], positions).astype(jnp.bfloat16)
    keys_new = rotate(projected[:, :, GROUP], positions).astype(jnp.bfloat16)
    values_new = projected[:, :, GROUP + 1].astype(jnp.bfloat16)
    new_pairs = jnp.concatenate([keys_new, values_new], -1)
    live_rows = (jnp.arange(prefix_kv.shape[0], dtype=jnp.int32) < prefix_counts[0] * BLK).astype(
        jnp.int32
    )
    targets = jnp.repeat(handoff_slots, BLK)
    half_rows = row_count // 2
    lower_queries = queries[:half_rows]
    upper_queries = queries[half_rows:]
    lower_pos = device * row_count + jnp.arange(half_rows, dtype=jnp.int32)
    upper_pos = device * row_count + half_rows + jnp.arange(half_rows, dtype=jnp.int32)
    begun = (fresh_state(half_rows, head_count), fresh_state(half_rows, head_count))
    pairs_in = lax.all_gather(prefix_kv, "ctx", axis=0, tiled=True)
    flags_in = lax.all_gather(live_rows, "ctx", axis=0, tiled=True)
    key_rows = pairs_in[..., :HEAD_DIM]
    value_rows = pairs_in[..., HEAD_DIM:]
    visible = jnp.broadcast_to((flags_in > 0)[None, :], (half_rows, flags_in.shape[0]))
    after_prefix = (
        advance(begun[0], lower_queries, key_rows, value_rows, visible),
        advance(begun[1], upper_queries, key_rows, value_rows, visible),
    )
    slot_count = 4 * (row_count // BLK)
    empty_cache = jnp.zeros((slot_count * BLK, head_count, 2 * HEAD_DIM), jnp.bfloat16)
    pairs_in = lax.all_gather(new_pairs, "ctx", axis=0, tiled=True)
    start_row = jnp.int32(0)
    key_rows = pairs_in[..., :HEAD_DIM]
    value_rows = pairs_in[..., HEAD_DIM:]
    key_pos = jnp.arange(pairs_in.shape[0], dtype=jnp.int32)

    def update(states_now, query_set, query_pos):

        def compute(inner_state):
            return advance(
                inner_state, query_set, key_rows, value_rows, key_pos[None, :] <= query_pos[:, None]
            )

        def unchanged(inner_state):
            return inner_state

        return lax.cond(start_row <= query_pos[-1], compute, unchanged, states_now)

    lower_state = update(after_prefix[0], lower_queries, lower_pos)
    upper_state = update(after_prefix[1], upper_queries, upper_pos)
    pairs_in = lax.all_gather(new_pairs, "ctx", axis=0, tiled=True)
    block_count = pairs_in.shape[0] // BLK
    slot_blocks = (
        lax.all_gather(targets, "ctx", axis=0, tiled=True).reshape(block_count, BLK)[:, 0]
        - device * slot_count
    )
    onehot = (slot_blocks[None, :] == jnp.arange(slot_count, dtype=jnp.int32)[:, None]).astype(
        jnp.bfloat16
    )
    placed_rows = jnp.dot(
        onehot, pairs_in.reshape(block_count, -1), preferred_element_type=jnp.float32
    ).astype(jnp.bfloat16)
    decode_rows = placed_rows.reshape(empty_cache.shape)
    lower_out = finish(lower_state)
    upper_out = finish(upper_state)
    return (jnp.concatenate([lower_out, upper_out], 0), decode_rows)


def solution(mesh):
    placed = (
        P(("groups", "ctx"), ("head", "section")),
        P(),
        P("ctx", ("head", "section")),
        P(("groups", "ctx"), ("head", "section"), None),
        P(("groups", "ctx")),
        P("groups"),
        P(("groups", "ctx")),
    )
    return jax.shard_map(
        local,
        mesh=mesh,
        in_specs=placed,
        out_specs=(
            P(("groups", "ctx"), ("head", "section")),
            P(("groups", "ctx"), ("head", "section"), None),
        ),
        check_vma=False,
    )
```

```python
import functools
import math

import jax
import jax.numpy as jnp
from jax import lax
from jax.experimental import pallas as pl
from jax.experimental.pallas import tpu as pltpu
from jax.sharding import PartitionSpec as P

HEAD_DIM = 128
GROUP = 8
BLK = 128
ROPE_BASE = 500000.0
NORM_EPS = 1e-05
CW = 640
MESH = pl.DeviceIdType.MESH


def kernel(
    n, nh, ns, wire,
    tok_ref, gain_ref, w_hbm, pre_hbm, meta_in, cos_ref, sin_ref,
    att_ref, dec_ref,
    ss, stage, xfull, w_ref, part, outb, recv, pre, newkv, meta, qbuf, sbuf,
    wsem, psem, ss_s, ss_r, st_s, x_s, x_r, rs_s, rs_r, pre_s, pre_r, new_s, new_r, meta_s, meta_r,
):
    c = lax.axis_index("ctx")
    h = lax.axis_index("head")
    s = lax.axis_index("section")
    nhs = nh * ns
    hs = h * ns + s
    r = n // nhs
    rows, width = tok_ref.shape
    fw = width // r
    heads = pre.shape[1]
    nch = part.shape[1]
    prow = pre.shape[2]
    f32 = jnp.float32

    def plane(offset):
        other = lax.rem(hs + offset, nhs)
        return {"head": other // ns, "section": lax.rem(other, ns)}

    def rcopy(src, dst, ssem, rsem, dev):
        return pltpu.make_async_remote_copy(
            src_ref=src, dst_ref=dst, send_sem=ssem, recv_sem=rsem,
            device_id=dev, device_id_type=MESH,
        )

    wcopy = pltpu.make_async_copy(w_hbm, w_ref, wsem)
    wcopy.start()
    pcopy = pltpu.make_async_copy(pre_hbm, pre.at[c], psem)
    pcopy.start()

    barrier = pltpu.get_barrier_semaphore()
    for o in range(1, n):
        pl.semaphore_signal(
            barrier, inc=1, device_id={"ctx": lax.rem(c + o, n)}, device_id_type=MESH
        )
    for o in range(1, nhs):
        pl.semaphore_signal(barrier, inc=1, device_id=plane(o), device_id_type=MESH)

    values = tok_ref[...].astype(f32)
    acc = jnp.zeros((rows, 128), f32)
    for j in range(width // 128):
        piece = values[:, j * 128:(j + 1) * 128]
        acc = acc + piece * piece
    ss[hs] = acc
    meta[c] = meta_in[...]
    pl.semaphore_wait(barrier, n - 1 + nhs - 1)

    def ss_copy(o):
        return rcopy(ss.at[hs], ss.at[hs], ss_s.at[o], ss_r.at[hs], plane(o))

    for o in range(1, nhs):
        ss_copy(o).start()

    def meta_copy(o):
        return rcopy(
            meta.at[c], meta.at[c], meta_s.at[o], meta_r.at[c], {"ctx": lax.rem(c + o, n)}
        )

    def pre_copy(o):
        return rcopy(
            pre.at[c], pre.at[c], pre_s.at[o], pre_r.at[c], {"ctx": lax.rem(c + o, n)}
        )

    def new_copy(o):
        return rcopy(
            newkv.at[c], newkv.at[c], new_s.at[o], new_r.at[c], {"ctx": lax.rem(c + o, n)}
        )

    for o in range(1, nhs):
        other = lax.rem(hs + o, nhs)
        rcopy(ss.at[other], ss.at[other], ss_s.at[o], ss_r.at[other], plane(o)).wait_recv()
    total_sq = ss[0]
    for i in range(1, nhs):
        total_sq = total_sq + ss[i]
    scale = lax.rsqrt(jnp.sum(total_sq, -1, keepdims=True) / (width * nhs) + NORM_EPS)
    gain = gain_ref[:, pl.ds(pl.multiple_of(hs * width, 128), width)]
    normed = (tok_ref[...].astype(f32) * scale * gain.astype(f32)).astype(jnp.bfloat16)

    def st_copy(j):
        return rcopy(stage.at[j], xfull.at[c], st_s.at[j], x_r.at[c], {"ctx": hs * r + j})

    for j in range(r):
        piece = normed[:, j * fw:(j + 1) * fw]

        @pl.when(hs * r + j == c)
        def _():
            xfull[c] = piece

        @pl.when(hs * r + j != c)
        def _():
            stage[j] = piece
            st_copy(j).start()

    for o in range(1, n):
        meta_copy(o).start()
    pcopy.wait()
    for o in range(1, n):
        pre_copy(o).start()

    root = c // r
    root_h = root // ns
    root_s = lax.rem(root, ns)
    is_root = hs == root

    def x_copy(d, o):
        dev = {"section": lax.rem(s + 1, ns)} if o == 0 else {"head": lax.rem(h + o, nh)}
        return rcopy(xfull.at[d], xfull.at[d], x_s.at[d, o], x_r.at[d], dev)

    def x_arrive(d):
        @pl.when(jnp.logical_or(jnp.logical_not(is_root), d != c))
        def _():
            x_copy(d, 0).wait_recv()

        @pl.when(s == root_s)
        def _():
            @pl.when(h == root_h)
            def _():
                for o in range(1, nh):
                    x_copy(d, o).start()

            x_copy(d, 0).start()

    def rs_copy(d, k, right):
        if right:
            return rcopy(
                outb.at[d, k], recv.at[d, k], rs_s.at[d, k], rs_r.at[d, k], {"ctx": c + 1}
            )
        slot = jnp.where(d == c - 1, n, d)
        return rcopy(
            outb.at[d, k], recv.at[slot, k], rs_s.at[d, k], rs_r.at[slot, k], {"ctx": c - 1}
        )

    def rs_arrive(slot, k):
        rcopy(
            outb.at[0, k], recv.at[slot, k], rs_s.at[0, k], rs_r.at[slot, k],
            {"ctx": lax.rem(c + 1, n)},
        ).wait_recv()

    def dot(d, k):
        return jnp.dot(
            xfull[d], w_ref[:, pl.ds(pl.multiple_of(k * CW, 128), CW)],
            preferred_element_type=f32,
        )

    wcopy.wait()

    def forward(d, right):
        @pl.loop(0, nch)
        def _(k):
            first = (c == 0) if right else (c == n - 1)

            @pl.when(first)
            def _():
                outb[d, k] = dot(d, k).astype(wire)

            @pl.when(jnp.logical_not(first))
            def _():
                own = dot(d, k)
                rs_arrive(d, k)
                outb[d, k] = (own + recv[d, k].astype(f32)).astype(wire)

            rs_copy(d, k, right).start()

    @pl.loop(0, n - 1)
    def _(t):
        @pl.when(n - 1 - t > c)
        def _():
            x_arrive(n - 1 - t)
            forward(n - 1 - t, True)

        @pl.when(t < c)
        def _():
            x_arrive(t)
            forward(t, False)

    x_arrive(c)

    @pl.loop(0, nch)
    def _(k):
        part[0, k] = dot(c, k)

    @pl.loop(0, nch)
    def _(k):
        @pl.when(c > 0)
        def _():
            rs_arrive(c, k)
            part[0, k] += recv[c, k].astype(f32)

        @pl.when(c < n - 1)
        def _():
            rs_arrive(n, k)
            part[0, k] += recv[n, k].astype(f32)

    cosines = cos_ref[...]
    sines = sin_ref[...]
    per = CW // HEAD_DIM

    def piece_of(g, j):
        i = g * (GROUP + 2) + j
        return part[0, i // per, :, (i % per) * HEAD_DIM:(i % per + 1) * HEAD_DIM]

    def turned(v):
        return v * cosines + pltpu.roll(v, HEAD_DIM // 2, 1) * sines

    for g in range(heads):
        newkv[c, g, :, :HEAD_DIM] = turned(piece_of(g, GROUP)).astype(jnp.bfloat16)
        newkv[c, g, :, HEAD_DIM:] = piece_of(g, GROUP + 1).astype(jnp.bfloat16)
    for o in range(1, n):
        new_copy(o).start()
    for g in range(heads):
        for j in range(GROUP):
            qbuf[g, j * rows:(j + 1) * rows] = turned(piece_of(g, j)).astype(jnp.bfloat16)

    for o in range(1, n):
        src = lax.rem(c + o, n)
        dev = {"ctx": src}
        rcopy(meta.at[src], meta.at[src], meta_s.at[o], meta_r.at[src], dev).wait_recv()
        rcopy(pre.at[src], pre.at[src], pre_s.at[o], pre_r.at[src], dev).wait_recv()
    for o in range(1, n):
        src = lax.rem(c + o, n)
        dev = {"ctx": src}
        rcopy(newkv.at[src], newkv.at[src], new_s.at[o], new_r.at[src], dev).wait_recv()

    tile = sbuf.shape[1]
    per_tile = tile // rows
    factor = 1.0 / math.sqrt(HEAD_DIM)
    nt = (((1,), (1,)), ((), ()))
    unroll = n <= 4

    @pl.loop(0, heads * GROUP // per_tile)
    def _(i):
        g = i // (GROUP // per_tile)
        jj = lax.rem(i, GROUP // per_tile)
        q = qbuf[g, pl.ds(pl.multiple_of(jj * tile, 128), tile)]

        def scores(b, top):
            sp = lax.dot_general(q, pre[b, g, :, :HEAD_DIM], nt, preferred_element_type=f32)
            count = meta[b, 0:1, :]
            for z in range(prow // BLK):
                piece = jnp.where(count > z, sp[:, z * BLK:(z + 1) * BLK] * factor, -1e30)
                sbuf[b, :, z * BLK:(z + 1) * BLK] = piece
                top = jnp.maximum(top, piece)
            sn = lax.dot_general(q, newkv[b, g, :, :HEAD_DIM], nt, preferred_element_type=f32)
            row = lax.broadcasted_iota(jnp.int32, (tile, BLK), 0) % rows + c * rows
            col = lax.broadcasted_iota(jnp.int32, (tile, BLK), 1) + b * BLK
            piece = jnp.where(col <= row, sn * factor, -1e30)
            sbuf[b, :, prow:] = piece
            return jnp.maximum(top, piece)

        top = lax.fori_loop(0, n, scores, jnp.full((tile, BLK), -1e30, f32), unroll=unroll)
        peak = jnp.max(top, -1, keepdims=True)

        def blend(b, state):
            lsum, acc = state
            w = jnp.exp(sbuf[b] - peak)
            for z in range(w.shape[1] // BLK):
                lsum = lsum + w[:, z * BLK:(z + 1) * BLK]
            wb = w.astype(jnp.bfloat16)
            acc = acc + jnp.dot(
                wb[:, :prow], pre[b, g, :, HEAD_DIM:], preferred_element_type=f32
            )
            acc = acc + jnp.dot(
                wb[:, prow:], newkv[b, g, :, HEAD_DIM:], preferred_element_type=f32
            )
            return lsum, acc

        lsum, acc = lax.fori_loop(
            0, n, blend,
            (jnp.zeros((tile, BLK), f32), jnp.zeros((tile, HEAD_DIM), f32)),
            unroll=unroll,
        )
        out = (acc / jnp.sum(lsum, -1, keepdims=True)).astype(jnp.bfloat16)
        for z in range(per_tile):
            col = pl.multiple_of((i * per_tile + z) * HEAD_DIM, 128)
            att_ref[:, pl.ds(col, HEAD_DIM)] = out[z * rows:(z + 1) * rows]

    slots = dec_ref.shape[1] // BLK
    for g in range(heads):
        for q in range(slots):
            def pick(b, now):
                hit = meta[b, 1:2, 0:1] == c * slots + q
                return jnp.where(hit, newkv[b, g].astype(f32), now)

            found = lax.fori_loop(
                0, n, pick, jnp.zeros((BLK, 2 * HEAD_DIM), f32), unroll=unroll
            )
            dec_ref[g, q * BLK:(q + 1) * BLK] = found.astype(jnp.bfloat16)

    for o in range(1, nhs):
        ss_copy(o).wait_send()
    for j in range(r):
        @pl.when(hs * r + j != c)
        def _():
            st_copy(j).wait_send()
    for o in range(1, n):
        meta_copy(o).wait_send()
        pre_copy(o).wait_send()
        new_copy(o).wait_send()

    @pl.when(s == root_s)
    def _():
        @pl.loop(0, n)
        def _(d):
            @pl.when(h == root_h)
            def _():
                for o in range(1, nh):
                    x_copy(d, o).wait_send()

            x_copy(d, 0).wait_send()

    @pl.loop(0, n)
    def _(d):
        @pl.loop(0, nch)
        def _(k):
            @pl.when(d > c)
            def _():
                rs_copy(d, k, True).wait_send()

            @pl.when(d < c)
            def _():
                rs_copy(d, k, False).wait_send()


def local(n, nh, ns, tokens, norm_gain, w_qkv, prefix_kv, prefix_counts, span_offset, handoff_slots):
    rows, width = tokens.shape
    heads = prefix_kv.shape[1]
    prow = prefix_kv.shape[0]
    nch = w_qkv.shape[1] // CW
    fw = w_qkv.shape[0]
    slots = prow // BLK
    c = lax.axis_index("ctx")
    half = HEAD_DIM // 2
    frequency = ROPE_BASE ** (-(jnp.arange(half, dtype=jnp.float32) * 2.0) / HEAD_DIM)
    positions = (
        span_offset[0] * BLK + c * rows + jnp.arange(rows, dtype=jnp.int32)
    ).astype(jnp.float32)
    angles = positions[:, None] * frequency[None, :]
    cosines = jnp.cos(angles)
    sines = jnp.sin(angles)
    cosines = jnp.concatenate([cosines, cosines], -1)
    sines = jnp.concatenate([-sines, sines], -1)
    meta = jnp.concatenate([
        jnp.broadcast_to(prefix_counts[:, None], (1, 128)),
        jnp.broadcast_to(handoff_slots[:, None], (7, 128)),
    ], 0)
    wire = jnp.float32
    bf16 = jnp.bfloat16
    nhs = nh * ns
    vmem = pl.BlockSpec(memory_space=pltpu.VMEM)
    hbm = pl.BlockSpec(memory_space=pl.ANY)
    tile = 256 if n <= 4 else 128
    dma = pltpu.SemaphoreType.DMA
    att, dec = pl.pallas_call(
        functools.partial(kernel, n, nh, ns, wire),
        out_shape=(
            jax.ShapeDtypeStruct((rows, heads * GROUP * HEAD_DIM), bf16),
            jax.ShapeDtypeStruct((heads, slots * BLK, 2 * HEAD_DIM), bf16),
        ),
        in_specs=[vmem, vmem, hbm, hbm, vmem, vmem, vmem],
        out_specs=(vmem, vmem),
        scratch_shapes=[
            pltpu.VMEM((nhs, rows, 128), jnp.float32),
            pltpu.VMEM((n // nhs, rows, fw), bf16),
            pltpu.VMEM((n, rows, fw), bf16),
            pltpu.VMEM(w_qkv.shape, bf16),
            pltpu.VMEM((1, nch, rows, CW), jnp.float32),
            pltpu.VMEM((n, nch, rows, CW), wire),
            pltpu.VMEM((n + 1, nch, rows, CW), wire),
            pltpu.VMEM((n, heads, prow, 2 * HEAD_DIM), bf16),
            pltpu.VMEM((n, heads, rows, 2 * HEAD_DIM), bf16),
            pltpu.VMEM((n, 8, 128), jnp.int32),
            pltpu.VMEM((heads, GROUP * rows, HEAD_DIM), bf16),
            pltpu.VMEM((n, tile, prow + rows), jnp.float32),
            dma, dma,
            dma((nhs,)), dma((nhs,)),
            dma((n // nhs,)),
            dma((n, nh)), dma((n,)),
            dma((n, nch)), dma((n + 1, nch)),
            dma((n,)), dma((n,)), dma((n,)), dma((n,)), dma((n,)), dma((n,)),
        ],
        compiler_params=pltpu.CompilerParams(
            collective_id=0, has_side_effects=True, vmem_limit_bytes=56 * 1024 * 1024
        ),
    )(
        tokens, norm_gain.reshape(1, -1), w_qkv, prefix_kv.transpose(1, 0, 2), meta,
        cosines, sines,
    )
    return att, dec.transpose(1, 0, 2)


def solution(mesh):
    placed = (
        P(("groups", "ctx"), ("head", "section")),
        P(),
        P("ctx", ("head", "section")),
        P(("groups", "ctx"), ("head", "section"), None),
        P(("groups", "ctx")),
        P("groups"),
        P(("groups", "ctx")),
    )
    return jax.shard_map(
        functools.partial(
            local, mesh.shape["ctx"], mesh.shape["head"], mesh.shape["section"]
        ),
        mesh=mesh,
        in_specs=placed,
        out_specs=(
            P(("groups", "ctx"), ("head", "section")),
            P(("groups", "ctx"), ("head", "section"), None),
        ),
        check_vma=False,
    )
```

```python
import functools
import math

import jax
import jax.numpy as jnp
from jax import lax
from jax.experimental import pallas as pl
from jax.experimental.pallas import tpu as pltpu
from jax.sharding import PartitionSpec as P

HEAD_DIM = 128
GROUP = 8
BLK = 128
ROPE_BASE = 500000.0
NORM_EPS = 1e-05
CW = 640
MESH = pl.DeviceIdType.MESH


def kernel(
    n, nh, ns, wire,
    tok_ref, gain_ref, w_hbm, pre_hbm, meta_in, cos_ref, sin_ref,
    att_ref, dec_ref,
    ss, stage, xfull, w_ref, part, outb, recv, pre, newkv, meta, qbuf, sbuf,
    wsem, psem, ss_s, ss_r, st_s, x_s, x_r, rs_s, rs_r, pre_s, pre_r, new_s, new_r, meta_s, meta_r,
):
    c = lax.axis_index("ctx")
    h = lax.axis_index("head")
    s = lax.axis_index("section")
    nhs = nh * ns
    hs = h * ns + s
    r = n // nhs
    rows, width = tok_ref.shape
    fw = width // r
    heads = pre.shape[1]
    nch = part.shape[1]
    prow = pre.shape[2]
    f32 = jnp.float32

    def plane(offset):
        other = lax.rem(hs + offset, nhs)
        return {"head": other // ns, "section": lax.rem(other, ns)}

    def rcopy(src, dst, ssem, rsem, dev):
        return pltpu.make_async_remote_copy(
            src_ref=src, dst_ref=dst, send_sem=ssem, recv_sem=rsem,
            device_id=dev, device_id_type=MESH,
        )

    wcopy = pltpu.make_async_copy(w_hbm, w_ref, wsem)
    wcopy.start()
    pcopy = pltpu.make_async_copy(pre_hbm, pre.at[c], psem)
    pcopy.start()

    barrier = pltpu.get_barrier_semaphore()
    for o in range(1, n * nh):
        other = lax.rem(c * nh + h + o, n * nh)
        pl.semaphore_signal(
            barrier, inc=1, device_id={"ctx": other // nh, "head": lax.rem(other, nh)},
            device_id_type=MESH,
        )
    for o in range(1, ns):
        for p in range(nh):
            pl.semaphore_signal(
                barrier, inc=1, device_id={"head": p, "section": lax.rem(s + o, ns)},
                device_id_type=MESH,
            )

    values = tok_ref[...].astype(f32)
    acc = jnp.zeros((rows, 128), f32)
    for j in range(width // 128):
        piece = values[:, j * 128:(j + 1) * 128]
        acc = acc + piece * piece
    ss[hs] = acc
    meta[c] = meta_in[...]
    pl.semaphore_wait(barrier, n * nh - 1 + (ns - 1) * nh)

    def ss_copy(o):
        return rcopy(ss.at[hs], ss.at[hs], ss_s.at[o], ss_r.at[hs], plane(o))

    for o in range(1, nhs):
        ss_copy(o).start()

    def meta_copy(o):
        return rcopy(
            meta.at[c], meta.at[c], meta_s.at[o], meta_r.at[c], {"ctx": lax.rem(c + o, n)}
        )

    def pre_copy(b, right):
        dev = {"ctx": c + 1} if right else {"ctx": c - 1}
        return rcopy(pre.at[b], pre.at[b], pre_s.at[int(right), b], pre_r.at[b], dev)

    def pre_send(b, right):
        @pl.when((c < n - 1) if right else (c > 0))
        def _():
            pre_copy(b, right).start()

    def pre_step(t):
        @pl.when(c - 1 - t >= 0)
        def _():
            pre_copy(c - 1 - t, False).wait_recv()
            pre_send(c - 1 - t, True)

        @pl.when(c + 1 + t <= n - 1)
        def _():
            pre_copy(c + 1 + t, True).wait_recv()
            pre_send(c + 1 + t, False)

    def new_copy(o, g):
        return rcopy(
            newkv.at[c, g], newkv.at[c, g], new_s.at[o, g], new_r.at[c, g],
            {"ctx": lax.rem(c + o, n)},
        )

    for o in range(1, nhs):
        other = lax.rem(hs + o, nhs)
        rcopy(ss.at[other], ss.at[other], ss_s.at[o], ss_r.at[other], plane(o)).wait_recv()
    total_sq = ss[0]
    for i in range(1, nhs):
        total_sq = total_sq + ss[i]
    scale = lax.rsqrt(jnp.sum(total_sq, -1, keepdims=True) / (width * nhs) + NORM_EPS)
    gain = gain_ref[:, pl.ds(pl.multiple_of(hs * width, 128), width)]
    normed = (tok_ref[...].astype(f32) * scale * gain.astype(f32)).astype(jnp.bfloat16)

    def st_copy(j, p):
        return rcopy(
            stage.at[j, p], xfull.at[c, p], st_s.at[j, p], x_r.at[c, p],
            {"ctx": hs * r + j, "head": p},
        )

    def here(j, p):
        return jnp.logical_and(hs * r + j == c, h == p)

    prt = rows // nh
    for j in range(r):
        for p in range(nh):
            piece = normed[p * prt:(p + 1) * prt, j * fw:(j + 1) * fw]

            @pl.when(here(j, p))
            def _():
                xfull[c, p] = piece

            @pl.when(jnp.logical_not(here(j, p)))
            def _():
                stage[j, p] = piece
                st_copy(j, p).start()

    for o in range(1, n):
        meta_copy(o).start()
    pcopy.wait()
    pre_send(c, True)
    pre_send(c, False)

    root = c // r
    root_s = lax.rem(root, ns)
    is_root = hs == root

    def x_copy(d, p, o):
        dev = {"section": lax.rem(s + 1, ns)} if o == 0 else {"head": lax.rem(h + o, nh)}
        return rcopy(xfull.at[d, p], xfull.at[d, p], x_s.at[d, p, o], x_r.at[d, p], dev)

    def x_arrive(d):
        @pl.when(jnp.logical_not(jnp.logical_and(is_root, d == c)))
        def _():
            x_copy(d, h, 0).wait_recv()

        @pl.when(s == root_s)
        def _():
            for o in range(1, nh):
                x_copy(d, h, o).start()
            x_copy(d, h, 0).start()

        for o in range(1, nh):
            p = lax.rem(h + o, nh)
            x_copy(d, p, 0).wait_recv()

            @pl.when(s == root_s)
            def _():
                x_copy(d, p, 0).start()

    def rs_copy(d, k, right):
        if right:
            return rcopy(
                outb.at[d, k], recv.at[d, k], rs_s.at[d, k], rs_r.at[d, k], {"ctx": c + 1}
            )
        slot = jnp.where(d == c - 1, n, d)
        return rcopy(
            outb.at[d, k], recv.at[slot, k], rs_s.at[d, k], rs_r.at[slot, k], {"ctx": c - 1}
        )

    def rs_arrive(slot, k):
        rcopy(
            outb.at[0, k], recv.at[slot, k], rs_s.at[0, k], rs_r.at[slot, k],
            {"ctx": lax.rem(c + 1, n)},
        ).wait_recv()

    def dot(d, k):
        return jnp.dot(
            xfull[d].reshape(rows, fw), w_ref[:, pl.ds(pl.multiple_of(k * CW, 128), CW)],
            preferred_element_type=f32,
        )

    wcopy.wait()

    per_head = nch // heads

    def forward(d, right, g):
        @pl.loop(g * per_head, (g + 1) * per_head)
        def _(k):
            first = (c == 0) if right else (c == n - 1)

            @pl.when(first)
            def _():
                outb[d, k] = dot(d, k).astype(wire)

            @pl.when(jnp.logical_not(first))
            def _():
                own = dot(d, k)
                rs_arrive(d, k)
                outb[d, k] = (own + recv[d, k].astype(f32)).astype(wire)

            rs_copy(d, k, right).start()

    for g in range(heads):
        @pl.loop(0, n - 1)
        def _(t):
            @pl.when(n - 1 - t > c)
            def _():
                if g == 0:
                    x_arrive(n - 1 - t)
                forward(n - 1 - t, True, g)

            @pl.when(t < c)
            def _():
                if g == 0:
                    x_arrive(t)
                forward(t, False, g)

            if g == heads - 1:
                pre_step(t)

        if g == 0:
            x_arrive(c)

    def own(g):
        @pl.loop(g * per_head, (g + 1) * per_head)
        def _(k):
            part[0, k] = dot(c, k)

    def collect(g):
        @pl.loop(g * per_head, (g + 1) * per_head)
        def _(k):
            @pl.when(c > 0)
            def _():
                rs_arrive(c, k)
                part[0, k] += recv[c, k].astype(f32)

            @pl.when(c < n - 1)
            def _():
                rs_arrive(n, k)
                part[0, k] += recv[n, k].astype(f32)

    cosines = cos_ref[...]
    sines = sin_ref[...]
    per = CW // HEAD_DIM

    def piece_of(g, j):
        i = g * (GROUP + 2) + j
        return part[0, i // per, :, (i % per) * HEAD_DIM:(i % per + 1) * HEAD_DIM]

    def turned(v):
        return v * cosines + pltpu.roll(v, HEAD_DIM // 2, 1) * sines

    def publish(g):
        newkv[c, g, :, :HEAD_DIM] = turned(piece_of(g, GROUP)).astype(jnp.bfloat16)
        newkv[c, g, :, HEAD_DIM:] = piece_of(g, GROUP + 1).astype(jnp.bfloat16)
        for o in range(1, n):
            new_copy(o, g).start()
        for j in range(GROUP):
            qbuf[g, j * rows:(j + 1) * rows] = turned(piece_of(g, j)).astype(jnp.bfloat16)

    def new_arrive(g):
        for o in range(1, n):
            src = lax.rem(c + o, n)
            rcopy(
                newkv.at[src, g], newkv.at[src, g], new_s.at[o, g], new_r.at[src, g],
                {"ctx": src},
            ).wait_recv()

    tile = sbuf.shape[1]
    per_tile = tile // rows
    factor = 1.0 / math.sqrt(HEAD_DIM)
    nt = (((1,), (1,)), ((), ()))
    unroll = n <= 4

    def one_tile(g, jj):
        i = g * (GROUP // per_tile) + jj
        q = qbuf[g, pl.ds(pl.multiple_of(jj * tile, 128), tile)]

        def scores(b, top):
            sp = lax.dot_general(q, pre[b, g, :, :HEAD_DIM], nt, preferred_element_type=f32)
            count = meta[b, 0:1, :]
            for z in range(prow // BLK):
                piece = jnp.where(count > z, sp[:, z * BLK:(z + 1) * BLK] * factor, -1e30)
                sbuf[b, :, z * BLK:(z + 1) * BLK] = piece
                top = jnp.maximum(top, piece)
            sn = lax.dot_general(q, newkv[b, g, :, :HEAD_DIM], nt, preferred_element_type=f32)
            row = lax.broadcasted_iota(jnp.int32, (tile, BLK), 0) % rows + c * rows
            col = lax.broadcasted_iota(jnp.int32, (tile, BLK), 1) + b * BLK
            piece = jnp.where(col <= row, sn * factor, -1e30)
            sbuf[b, :, prow:] = piece
            return jnp.maximum(top, piece)

        top = lax.fori_loop(0, n, scores, jnp.full((tile, BLK), -1e30, f32), unroll=unroll)
        peak = jnp.max(top, -1, keepdims=True)

        def blend(b, state):
            lsum, acc = state
            w = jnp.exp(sbuf[b] - peak)
            for z in range(w.shape[1] // BLK):
                lsum = lsum + w[:, z * BLK:(z + 1) * BLK]
            wb = w.astype(jnp.bfloat16)
            acc = acc + jnp.dot(
                wb[:, :prow], pre[b, g, :, HEAD_DIM:], preferred_element_type=f32
            )
            acc = acc + jnp.dot(
                wb[:, prow:], newkv[b, g, :, HEAD_DIM:], preferred_element_type=f32
            )
            return lsum, acc

        lsum, acc = lax.fori_loop(
            0, n, blend,
            (jnp.zeros((tile, BLK), f32), jnp.zeros((tile, HEAD_DIM), f32)),
            unroll=unroll,
        )
        out = (acc / jnp.sum(lsum, -1, keepdims=True)).astype(jnp.bfloat16)
        for z in range(per_tile):
            col = pl.multiple_of((i * per_tile + z) * HEAD_DIM, 128)
            att_ref[:, pl.ds(col, HEAD_DIM)] = out[z * rows:(z + 1) * rows]

    slots = dec_ref.shape[1] // BLK

    def attend(g):
        @pl.loop(0, GROUP // per_tile)
        def _(jj):
            one_tile(g, jj)

    def place(g):
        for q in range(slots):
            def pick(b, now):
                hit = meta[b, 1:2, 0:1] == c * slots + q
                return jnp.where(hit, newkv[b, g].astype(f32), now)

            found = lax.fori_loop(
                0, n, pick, jnp.zeros((BLK, 2 * HEAD_DIM), f32), unroll=unroll
            )
            dec_ref[g, q * BLK:(q + 1) * BLK] = found.astype(jnp.bfloat16)

    for o in range(1, n):
        src = lax.rem(c + o, n)
        rcopy(
            meta.at[src], meta.at[src], meta_s.at[o], meta_r.at[src], {"ctx": src}
        ).wait_recv()
    own(0)
    collect(0)
    publish(0)
    for g in range(1, heads):
        own(g)
        new_arrive(g - 1)
        attend(g - 1)
        collect(g)
        publish(g)
        place(g - 1)
    new_arrive(heads - 1)
    attend(heads - 1)
    place(heads - 1)

    for o in range(1, nhs):
        ss_copy(o).wait_send()
    for j in range(r):
        for p in range(nh):
            @pl.when(jnp.logical_not(here(j, p)))
            def _():
                st_copy(j, p).wait_send()
    for o in range(1, n):
        meta_copy(o).wait_send()
        for g in range(heads):
            new_copy(o, g).wait_send()

    @pl.loop(0, n)
    def _(b):
        @pl.when(jnp.logical_and(b <= c, c < n - 1))
        def _():
            pre_copy(b, True).wait_send()

        @pl.when(jnp.logical_and(b >= c, c > 0))
        def _():
            pre_copy(b, False).wait_send()

    @pl.when(s == root_s)
    def _():
        @pl.loop(0, n)
        def _(d):
            for o in range(1, nh):
                x_copy(d, h, o).wait_send()
            for p in range(nh):
                x_copy(d, p, 0).wait_send()

    @pl.loop(0, n)
    def _(d):
        @pl.loop(0, nch)
        def _(k):
            @pl.when(d > c)
            def _():
                rs_copy(d, k, True).wait_send()

            @pl.when(d < c)
            def _():
                rs_copy(d, k, False).wait_send()


def local(n, nh, ns, tokens, norm_gain, w_qkv, prefix_kv, prefix_counts, span_offset, handoff_slots):
    rows, width = tokens.shape
    heads = prefix_kv.shape[1]
    prow = prefix_kv.shape[0]
    nch = w_qkv.shape[1] // CW
    fw = w_qkv.shape[0]
    slots = prow // BLK
    c = lax.axis_index("ctx")
    half = HEAD_DIM // 2
    frequency = ROPE_BASE ** (-(jnp.arange(half, dtype=jnp.float32) * 2.0) / HEAD_DIM)
    positions = (
        span_offset[0] * BLK + c * rows + jnp.arange(rows, dtype=jnp.int32)
    ).astype(jnp.float32)
    angles = positions[:, None] * frequency[None, :]
    cosines = jnp.cos(angles)
    sines = jnp.sin(angles)
    cosines = jnp.concatenate([cosines, cosines], -1)
    sines = jnp.concatenate([-sines, sines], -1)
    meta = jnp.concatenate([
        jnp.broadcast_to(prefix_counts[:, None], (1, 128)),
        jnp.broadcast_to(handoff_slots[:, None], (7, 128)),
    ], 0)
    wire = jnp.float32
    bf16 = jnp.bfloat16
    nhs = nh * ns
    vmem = pl.BlockSpec(memory_space=pltpu.VMEM)
    hbm = pl.BlockSpec(memory_space=pl.ANY)
    tile = 256 if n <= 4 else 128
    dma = pltpu.SemaphoreType.DMA
    att, dec = pl.pallas_call(
        functools.partial(kernel, n, nh, ns, wire),
        out_shape=(
            jax.ShapeDtypeStruct((rows, heads * GROUP * HEAD_DIM), bf16),
            jax.ShapeDtypeStruct((heads, slots * BLK, 2 * HEAD_DIM), bf16),
        ),
        in_specs=[vmem, vmem, hbm, hbm, vmem, vmem, vmem],
        out_specs=(vmem, vmem),
        scratch_shapes=[
            pltpu.VMEM((nhs, rows, 128), jnp.float32),
            pltpu.VMEM((n // nhs, nh, rows // nh, fw), bf16),
            pltpu.VMEM((n, nh, rows // nh, fw), bf16),
            pltpu.VMEM(w_qkv.shape, bf16),
            pltpu.VMEM((1, nch, rows, CW), jnp.float32),
            pltpu.VMEM((n, nch, rows, CW), wire),
            pltpu.VMEM((n + 1, nch, rows, CW), wire),
            pltpu.VMEM((n, heads, prow, 2 * HEAD_DIM), bf16),
            pltpu.VMEM((n, heads, rows, 2 * HEAD_DIM), bf16),
            pltpu.VMEM((n, 8, 128), jnp.int32),
            pltpu.VMEM((heads, GROUP * rows, HEAD_DIM), bf16),
            pltpu.VMEM((n, tile, prow + rows), jnp.float32),
            dma, dma,
            dma((nhs,)), dma((nhs,)),
            dma((n // nhs, nh)),
            dma((n, nh, nh)), dma((n, nh)),
            dma((n, nch)), dma((n + 1, nch)),
            dma((2, n)), dma((n,)), dma((n, heads)), dma((n, heads)), dma((n,)), dma((n,)),
        ],
        compiler_params=pltpu.CompilerParams(
            collective_id=0, has_side_effects=True, vmem_limit_bytes=56 * 1024 * 1024
        ),
    )(
        tokens, norm_gain.reshape(1, -1), w_qkv, prefix_kv.transpose(1, 0, 2), meta,
        cosines, sines,
    )
    return att, dec.transpose(1, 0, 2)


def solution(mesh):
    placed = (
        P(("groups", "ctx"), ("head", "section")),
        P(),
        P("ctx", ("head", "section")),
        P(("groups", "ctx"), ("head", "section"), None),
        P(("groups", "ctx")),
        P("groups"),
        P(("groups", "ctx")),
    )
    return jax.shard_map(
        functools.partial(
            local, mesh.shape["ctx"], mesh.shape["head"], mesh.shape["section"]
        ),
        mesh=mesh,
        in_specs=placed,
        out_specs=(
            P(("groups", "ctx"), ("head", "section")),
            P(("groups", "ctx"), ("head", "section"), None),
        ),
        check_vma=False,
    )
```

```python
import functools
import math

import jax
import jax.numpy as jnp
from jax import lax
from jax.experimental import pallas as pl
from jax.experimental.pallas import tpu as pltpu
from jax.sharding import PartitionSpec as P

HEAD_DIM = 128
GROUP = 8
BLK = 128
ROPE_BASE = 500000.0
NORM_EPS = 1e-05
CW = 256
MESH = pl.DeviceIdType.MESH


def kernel(
    n, nh, ns, wire,
    tok_ref, gain_ref, w_hbm, pre_hbm, meta_in, cos_ref, sin_ref,
    att_ref, dec_ref,
    ss, stage, xfull, w_ref, part, outb, recv, pre, newkv, meta, qbuf, sbuf,
    wsem, psem, ss_s, ss_r, st_s, x_s, x_r, rs_s, rs_r, pre_s, pre_r, new_s, new_r, meta_s, meta_r,
):
    c = lax.axis_index("ctx")
    h = lax.axis_index("head")
    s = lax.axis_index("section")
    nhs = nh * ns
    hs = h * ns + s
    r = n // nhs
    rows, width = tok_ref.shape
    fw = width // r
    heads = pre.shape[1]
    nch = part.shape[1]
    prow = pre.shape[2]
    f32 = jnp.float32

    def plane(offset):
        other = lax.rem(hs + offset, nhs)
        return {"head": other // ns, "section": lax.rem(other, ns)}

    def rcopy(src, dst, ssem, rsem, dev):
        return pltpu.make_async_remote_copy(
            src_ref=src, dst_ref=dst, send_sem=ssem, recv_sem=rsem,
            device_id=dev, device_id_type=MESH,
        )

    wcopy = pltpu.make_async_copy(w_hbm, w_ref, wsem)
    wcopy.start()
    pcopy = pltpu.make_async_copy(pre_hbm, pre.at[c], psem)
    pcopy.start()

    barrier = pltpu.get_barrier_semaphore()
    for o in range(1, n * nh):
        other = lax.rem(c * nh + h + o, n * nh)
        pl.semaphore_signal(
            barrier, inc=1, device_id={"ctx": other // nh, "head": lax.rem(other, nh)},
            device_id_type=MESH,
        )
    for o in range(1, ns):
        for p in range(nh):
            pl.semaphore_signal(
                barrier, inc=1, device_id={"head": p, "section": lax.rem(s + o, ns)},
                device_id_type=MESH,
            )

    values = tok_ref[...].astype(f32)
    acc = jnp.zeros((rows, 128), f32)
    for j in range(width // 128):
        piece = values[:, j * 128:(j + 1) * 128]
        acc = acc + piece * piece
    ss[hs] = acc
    meta[c] = meta_in[...]
    pl.semaphore_wait(barrier, n * nh - 1 + (ns - 1) * nh)

    def ss_copy(o):
        return rcopy(ss.at[hs], ss.at[hs], ss_s.at[o], ss_r.at[hs], plane(o))

    for o in range(1, nhs):
        ss_copy(o).start()

    def meta_copy(o):
        return rcopy(
            meta.at[c], meta.at[c], meta_s.at[o], meta_r.at[c], {"ctx": lax.rem(c + o, n)}
        )

    def pre_copy(b, right):
        dev = {"ctx": c + 1} if right else {"ctx": c - 1}
        return rcopy(pre.at[b], pre.at[b], pre_s.at[int(right), b], pre_r.at[b], dev)

    def pre_send(b, right):
        @pl.when((c < n - 1) if right else (c > 0))
        def _():
            pre_copy(b, right).start()

    def pre_step(t):
        @pl.when(c - 1 - t >= 0)
        def _():
            pre_copy(c - 1 - t, False).wait_recv()
            pre_send(c - 1 - t, True)

        @pl.when(c + 1 + t <= n - 1)
        def _():
            pre_copy(c + 1 + t, True).wait_recv()
            pre_send(c + 1 + t, False)

    def new_copy(o, g):
        return rcopy(
            newkv.at[c, g], newkv.at[c, g], new_s.at[o, g], new_r.at[c, g],
            {"ctx": lax.rem(c + o, n)},
        )

    for o in range(1, nhs):
        other = lax.rem(hs + o, nhs)
        rcopy(ss.at[other], ss.at[other], ss_s.at[o], ss_r.at[other], plane(o)).wait_recv()
    total_sq = ss[0]
    for i in range(1, nhs):
        total_sq = total_sq + ss[i]
    scale = lax.rsqrt(jnp.sum(total_sq, -1, keepdims=True) / (width * nhs) + NORM_EPS)
    gain = gain_ref[:, pl.ds(pl.multiple_of(hs * width, 128), width)]
    normed = (tok_ref[...].astype(f32) * scale * gain.astype(f32)).astype(jnp.bfloat16)

    def st_copy(j, p):
        return rcopy(
            stage.at[j, p], xfull.at[c, p], st_s.at[j, p], x_r.at[c, p],
            {"ctx": hs * r + j, "head": p},
        )

    def here(j, p):
        return jnp.logical_and(hs * r + j == c, h == p)

    prt = rows // nh
    for j in range(r):
        for p in range(nh):
            piece = normed[p * prt:(p + 1) * prt, j * fw:(j + 1) * fw]

            @pl.when(here(j, p))
            def _():
                xfull[c, p] = piece

            @pl.when(jnp.logical_not(here(j, p)))
            def _():
                stage[j, p] = piece
                st_copy(j, p).start()

    for o in range(1, n):
        meta_copy(o).start()
    pcopy.wait()
    pre_send(c, True)
    pre_send(c, False)

    root = c // r
    root_s = lax.rem(root, ns)
    is_root = hs == root

    def x_copy(d, p, o):
        dev = {"section": lax.rem(s + 1, ns)} if o == 0 else {"head": lax.rem(h + o, nh)}
        return rcopy(xfull.at[d, p], xfull.at[d, p], x_s.at[d, p, o], x_r.at[d, p], dev)

    def x_arrive(d):
        @pl.when(jnp.logical_not(jnp.logical_and(is_root, d == c)))
        def _():
            x_copy(d, h, 0).wait_recv()

        @pl.when(s == root_s)
        def _():
            for o in range(1, nh):
                x_copy(d, h, o).start()
            x_copy(d, h, 0).start()

        for o in range(1, nh):
            p = lax.rem(h + o, nh)
            x_copy(d, p, 0).wait_recv()

            @pl.when(s == root_s)
            def _():
                x_copy(d, p, 0).start()

    def rs_copy(d, k, right):
        if right:
            return rcopy(
                outb.at[d, k], recv.at[d, k], rs_s.at[d, k], rs_r.at[d, k], {"ctx": c + 1}
            )
        slot = jnp.where(d == c - 1, n, d)
        return rcopy(
            outb.at[d, k], recv.at[slot, k], rs_s.at[d, k], rs_r.at[slot, k], {"ctx": c - 1}
        )

    def rs_arrive(slot, k):
        rcopy(
            outb.at[0, k], recv.at[slot, k], rs_s.at[0, k], rs_r.at[slot, k],
            {"ctx": lax.rem(c + 1, n)},
        ).wait_recv()

    def dot(d, k):
        return jnp.dot(
            xfull[d].reshape(rows, fw), w_ref[:, pl.ds(pl.multiple_of(k * CW, 128), CW)],
            preferred_element_type=f32,
        )

    wcopy.wait()

    per_head = nch // heads

    def forward(d, right, g):
        @pl.loop(g * per_head, (g + 1) * per_head)
        def _(k):
            first = (c == 0) if right else (c == n - 1)

            @pl.when(first)
            def _():
                outb[d, k] = dot(d, k).astype(wire)

            @pl.when(jnp.logical_not(first))
            def _():
                own = dot(d, k)
                rs_arrive(d, k)
                outb[d, k] = (own + recv[d, k].astype(f32)).astype(wire)

            rs_copy(d, k, right).start()

    for g in range(heads):
        @pl.loop(0, n - 1)
        def _(t):
            @pl.when(n - 1 - t > c)
            def _():
                if g == 0:
                    x_arrive(n - 1 - t)
                forward(n - 1 - t, True, g)

            @pl.when(t < c)
            def _():
                if g == 0:
                    x_arrive(t)
                forward(t, False, g)

            if g == heads - 1:
                pre_step(t)

        if g == 0:
            x_arrive(c)

    def own(g):
        @pl.loop(g * per_head, (g + 1) * per_head)
        def _(k):
            part[0, k] = dot(c, k)

    def collect(g):
        @pl.loop(g * per_head, (g + 1) * per_head)
        def _(k):
            @pl.when(c > 0)
            def _():
                rs_arrive(c, k)
                part[0, k] += recv[c, k].astype(f32)

            @pl.when(c < n - 1)
            def _():
                rs_arrive(n, k)
                part[0, k] += recv[n, k].astype(f32)

    cosines = cos_ref[...]
    sines = sin_ref[...]
    per = CW // HEAD_DIM

    def piece_of(g, j):
        i = g * (GROUP + 2) + j
        return part[0, i // per, :, (i % per) * HEAD_DIM:(i % per + 1) * HEAD_DIM]

    def turned(v):
        return v * cosines + pltpu.roll(v, HEAD_DIM // 2, 1) * sines

    def publish(g):
        newkv[c, g, :, :HEAD_DIM] = turned(piece_of(g, GROUP)).astype(jnp.bfloat16)
        newkv[c, g, :, HEAD_DIM:] = piece_of(g, GROUP + 1).astype(jnp.bfloat16)
        for o in range(1, n):
            new_copy(o, g).start()
        for j in range(GROUP):
            qbuf[g, j * rows:(j + 1) * rows] = turned(piece_of(g, j)).astype(jnp.bfloat16)

    def new_arrive(g):
        for o in range(1, n):
            src = lax.rem(c + o, n)
            rcopy(
                newkv.at[src, g], newkv.at[src, g], new_s.at[o, g], new_r.at[src, g],
                {"ctx": src},
            ).wait_recv()

    tile = sbuf.shape[1]
    per_tile = tile // rows
    factor = 1.0 / math.sqrt(HEAD_DIM)
    nt = (((1,), (1,)), ((), ()))
    unroll = n <= 4

    def one_tile(g, jj):
        i = g * (GROUP // per_tile) + jj
        q = qbuf[g, pl.ds(pl.multiple_of(jj * tile, 128), tile)]

        def scores(b, top):
            sp = lax.dot_general(q, pre[b, g, :, :HEAD_DIM], nt, preferred_element_type=f32)
            count = meta[b, 0:1, :]
            for z in range(prow // BLK):
                piece = jnp.where(count > z, sp[:, z * BLK:(z + 1) * BLK] * factor, -1e30)
                sbuf[b, :, z * BLK:(z + 1) * BLK] = piece
                top = jnp.maximum(top, piece)
            sn = lax.dot_general(q, newkv[b, g, :, :HEAD_DIM], nt, preferred_element_type=f32)
            row = lax.broadcasted_iota(jnp.int32, (tile, BLK), 0) % rows + c * rows
            col = lax.broadcasted_iota(jnp.int32, (tile, BLK), 1) + b * BLK
            piece = jnp.where(col <= row, sn * factor, -1e30)
            sbuf[b, :, prow:] = piece
            return jnp.maximum(top, piece)

        top = lax.fori_loop(0, n, scores, jnp.full((tile, BLK), -1e30, f32), unroll=unroll)
        peak = jnp.max(top, -1, keepdims=True)

        def blend(b, state):
            lsum, acc = state
            w = jnp.exp(sbuf[b] - peak)
            for z in range(w.shape[1] // BLK):
                lsum = lsum + w[:, z * BLK:(z + 1) * BLK]
            wb = w.astype(jnp.bfloat16)
            acc = acc + jnp.dot(
                wb[:, :prow], pre[b, g, :, HEAD_DIM:], preferred_element_type=f32
            )
            acc = acc + jnp.dot(
                wb[:, prow:], newkv[b, g, :, HEAD_DIM:], preferred_element_type=f32
            )
            return lsum, acc

        lsum, acc = lax.fori_loop(
            0, n, blend,
            (jnp.zeros((tile, BLK), f32), jnp.zeros((tile, HEAD_DIM), f32)),
            unroll=unroll,
        )
        out = (acc / jnp.sum(lsum, -1, keepdims=True)).astype(jnp.bfloat16)
        for z in range(per_tile):
            col = pl.multiple_of((i * per_tile + z) * HEAD_DIM, 128)
            att_ref[:, pl.ds(col, HEAD_DIM)] = out[z * rows:(z + 1) * rows]

    slots = dec_ref.shape[1] // BLK

    def attend(g):
        @pl.loop(0, GROUP // per_tile)
        def _(jj):
            one_tile(g, jj)

    def place(g):
        for q in range(slots):
            def pick(b, now):
                hit = meta[b, 1:2, 0:1] == c * slots + q
                return jnp.where(hit, newkv[b, g].astype(f32), now)

            found = lax.fori_loop(
                0, n, pick, jnp.zeros((BLK, 2 * HEAD_DIM), f32), unroll=unroll
            )
            dec_ref[g, q * BLK:(q + 1) * BLK] = found.astype(jnp.bfloat16)

    for o in range(1, n):
        src = lax.rem(c + o, n)
        rcopy(
            meta.at[src], meta.at[src], meta_s.at[o], meta_r.at[src], {"ctx": src}
        ).wait_recv()
    own(0)
    collect(0)
    publish(0)
    for g in range(1, heads):
        own(g)
        new_arrive(g - 1)
        attend(g - 1)
        collect(g)
        publish(g)
        place(g - 1)
    new_arrive(heads - 1)
    attend(heads - 1)
    place(heads - 1)

    for o in range(1, nhs):
        ss_copy(o).wait_send()
    for j in range(r):
        for p in range(nh):
            @pl.when(jnp.logical_not(here(j, p)))
            def _():
                st_copy(j, p).wait_send()
    for o in range(1, n):
        meta_copy(o).wait_send()
        for g in range(heads):
            new_copy(o, g).wait_send()

    @pl.loop(0, n)
    def _(b):
        @pl.when(jnp.logical_and(b <= c, c < n - 1))
        def _():
            pre_copy(b, True).wait_send()

        @pl.when(jnp.logical_and(b >= c, c > 0))
        def _():
            pre_copy(b, False).wait_send()

    @pl.when(s == root_s)
    def _():
        @pl.loop(0, n)
        def _(d):
            for o in range(1, nh):
                x_copy(d, h, o).wait_send()
            for p in range(nh):
                x_copy(d, p, 0).wait_send()

    @pl.loop(0, n)
    def _(d):
        @pl.loop(0, nch)
        def _(k):
            @pl.when(d > c)
            def _():
                rs_copy(d, k, True).wait_send()

            @pl.when(d < c)
            def _():
                rs_copy(d, k, False).wait_send()


def local(n, nh, ns, tokens, norm_gain, w_qkv, prefix_kv, prefix_counts, span_offset, handoff_slots):
    rows, width = tokens.shape
    heads = prefix_kv.shape[1]
    prow = prefix_kv.shape[0]
    nch = w_qkv.shape[1] // CW
    fw = w_qkv.shape[0]
    slots = prow // BLK
    c = lax.axis_index("ctx")
    half = HEAD_DIM // 2
    frequency = ROPE_BASE ** (-(jnp.arange(half, dtype=jnp.float32) * 2.0) / HEAD_DIM)
    positions = (
        span_offset[0] * BLK + c * rows + jnp.arange(rows, dtype=jnp.int32)
    ).astype(jnp.float32)
    angles = positions[:, None] * frequency[None, :]
    cosines = jnp.cos(angles)
    sines = jnp.sin(angles)
    cosines = jnp.concatenate([cosines, cosines], -1)
    sines = jnp.concatenate([-sines, sines], -1)
    meta = jnp.concatenate([
        jnp.broadcast_to(prefix_counts[:, None], (1, 128)),
        jnp.broadcast_to(handoff_slots[:, None], (7, 128)),
    ], 0)
    wire = jnp.float32
    bf16 = jnp.bfloat16
    nhs = nh * ns
    vmem = pl.BlockSpec(memory_space=pltpu.VMEM)
    hbm = pl.BlockSpec(memory_space=pl.ANY)
    tile = 256 if n <= 4 else 128
    dma = pltpu.SemaphoreType.DMA
    att, dec = pl.pallas_call(
        functools.partial(kernel, n, nh, ns, wire),
        out_shape=(
            jax.ShapeDtypeStruct((rows, heads * GROUP * HEAD_DIM), bf16),
            jax.ShapeDtypeStruct((heads, slots * BLK, 2 * HEAD_DIM), bf16),
        ),
        in_specs=[vmem, vmem, hbm, hbm, vmem, vmem, vmem],
        out_specs=(vmem, vmem),
        scratch_shapes=[
            pltpu.VMEM((nhs, rows, 128), jnp.float32),
            pltpu.VMEM((n // nhs, nh, rows // nh, fw), bf16),
            pltpu.VMEM((n, nh, rows // nh, fw), bf16),
            pltpu.VMEM(w_qkv.shape, bf16),
            pltpu.VMEM((1, nch, rows, CW), jnp.float32),
            pltpu.VMEM((n, nch, rows, CW), wire),
            pltpu.VMEM((n + 1, nch, rows, CW), wire),
            pltpu.VMEM((n, heads, prow, 2 * HEAD_DIM), bf16),
            pltpu.VMEM((n, heads, rows, 2 * HEAD_DIM), bf16),
            pltpu.VMEM((n, 8, 128), jnp.int32),
            pltpu.VMEM((heads, GROUP * rows, HEAD_DIM), bf16),
            pltpu.VMEM((n, tile, prow + rows), jnp.float32),
            dma, dma,
            dma((nhs,)), dma((nhs,)),
            dma((n // nhs, nh)),
            dma((n, nh, nh)), dma((n, nh)),
            dma((n, nch)), dma((n + 1, nch)),
            dma((2, n)), dma((n,)), dma((n, heads)), dma((n, heads)), dma((n,)), dma((n,)),
        ],
        compiler_params=pltpu.CompilerParams(
            collective_id=0, has_side_effects=True, vmem_limit_bytes=56 * 1024 * 1024
        ),
    )(
        tokens, norm_gain.reshape(1, -1), w_qkv, prefix_kv.transpose(1, 0, 2), meta,
        cosines, sines,
    )
    return att, dec.transpose(1, 0, 2)


def solution(mesh):
    placed = (
        P(("groups", "ctx"), ("head", "section")),
        P(),
        P("ctx", ("head", "section")),
        P(("groups", "ctx"), ("head", "section"), None),
        P(("groups", "ctx")),
        P("groups"),
        P(("groups", "ctx")),
    )
    return jax.shard_map(
        functools.partial(
            local, mesh.shape["ctx"], mesh.shape["head"], mesh.shape["section"]
        ),
        mesh=mesh,
        in_specs=placed,
        out_specs=(
            P(("groups", "ctx"), ("head", "section")),
            P(("groups", "ctx"), ("head", "section"), None),
        ),
        check_vma=False,
    )
```
